1024 devices in a mesh: dp: 256 (over y, z, core), tp: 4 (over x).
Axes of the slice: x: 4, y: 8, z: 16, core: 2. Of those that a mesh axis runs over, the one named last changes fastest.
Arguments:
- hidden: bfloat16 [256, 128, 7168], P('dp', None, 'tp'), may hold values from -6 to 6
- routes: int32 [256, 1], P('dp'), may hold values from 0 to 2, as said below
- counts: int32 [256, 1], P('dp'), may hold values from 64 to 128
- gain_in: float32 [7168], P('tp'), may hold values from 0.1 to 1.9
- kv_down: bfloat16 [7168, 256], P('tp'), may hold values from -0.0625 to 0.0625
- gain_latent: float32 [256], replicated, may hold values from 0.1 to 1.9
- cotangent: bfloat16 [256, 3, 1, 128, 256], P('dp'), may hold values from -0.25 to 0.25
Outputs:
- latent: bfloat16 [256, 3, 1, 128, 256], P('dp')
- gradient: float32 [256, 7168], P('dp', 'tp')
The draws below stay inside these ranges and needn't reach their ends.
Inputs may be any that keep to these rules, and one draw needn't show every extreme that they name: `routes`: every offset sends a panel's trainer to a server at most 2 places further along dp, wrapping around; loads over trainers are uneven.
All inputs are finite; a program needn't handle non-finite values.
Results may differ from the reference program's by a relative error of at most 0.005.
Values may be sent and summed in bfloat16 or wider, within the bound.
No kernel may reach another device: no remote copies, remote signals or barrier semaphores. Data moves between devices by JAX's collectives and lax.ppermute only.
A program may use at most 32 MiB of HBM per device.

```python
import jax
import jax.numpy as jnp
from jax import lax

D = 7168
KV = 256
PANEL = 128
SLOTS = 1
REACH = 3
GROUPS = 256
PANELS = 256


def draw_routes(key, part):
    key = jax.random.fold_in(key, 11)
    first_key, second_key = jax.random.split(key)
    server = lax.broadcasted_iota(jnp.int32, (GROUPS, SLOTS), 0)
    aligned = (GROUPS - 1 - server) % REACH
    aligned = jnp.where(server == GROUPS - 1, 1 % REACH, aligned)
    spread_out = jax.random.randint(first_key, (GROUPS, SLOTS), 0, REACH)
    picker = jax.random.randint(second_key, (GROUPS, SLOTS), 0, 4)
    forced = server >= GROUPS - 3
    return jnp.where(forced | (picker < 2), aligned, spread_out).astype(jnp.int32)


def plant(values, rng, least, high):
    index_at = [jax.random.randint(jax.random.fold_in(rng, axis), (), 0, length) for axis, length in enumerate(values.shape)]
    widest = values.shape.index(max(values.shape))
    next_to = index_at[:widest] + [(index_at[widest] + 1) % values.shape[widest]] + index_at[widest + 1:]
    return values.at[tuple(index_at)].set(least).at[tuple(next_to)].set(high)


def with_spikes(array, rng, source, target, shards_of, factor):
    owner, partner = [(jnp.arange(array.shape[dim]) // (array.shape[dim] // shards_of)).reshape([-1 if axis == dim else 1 for axis in range(array.ndim)]) for dim in (source, target)]
    chosen = jax.random.permutation(rng, shards_of)[partner]
    strong = (owner == chosen) | (owner == (partner + shards_of // 2) % shards_of)
    return jnp.where(strong, factor * array, array)


def block_levels(key, extent, cuts, least, top_value):
    gain = 1.0
    for axis_at, shards_of in cuts:
        steps = jax.random.uniform(jax.random.fold_in(jax.random.fold_in(key, 6), axis_at), (shards_of,), jnp.float32, least / len(cuts), top_value / len(cuts))
        gain = gain * jnp.repeat(jnp.exp(steps), extent[axis_at] // shards_of).reshape((-1,) + (1,) * (len(extent) - 1 - axis_at))
    return gain


def gaussian(key, extent, spread, reach, cuts=(), kind=jnp.bfloat16):
    result = spread * jax.random.normal(key, extent, jnp.float32)
    if cuts:
        result = result * block_levels(key, extent, cuts, -0.22, 0.18)
    return jnp.clip(result, -reach, reach).astype(kind)


def heavy_noise(rng, shape, width, most, cuts, heavy, held_as=jnp.bfloat16):
    drawn = width * jax.random.normal(rng, shape, jnp.float32)
    if cuts:
        drawn = drawn * block_levels(rng, shape, cuts, -0.22, 0.18)
    return jnp.clip(with_spikes(drawn, jax.random.fold_in(rng, 3), *heavy), -most, most).astype(held_as)


def setup_inputs(seed: int = 0) -> dict:
    arg_keys = jax.random.split(jax.random.key(seed), 8)
    return {
        "hidden": gaussian(arg_keys[0], (PANELS, PANEL, D), 1.0, 6.0, ((0, 256), (2, 4))),
        "routes": draw_routes(jax.random.fold_in(arg_keys[7], 71), 0),
        "counts": plant(jax.random.randint(arg_keys[2], (GROUPS, SLOTS), PANEL // 2, PANEL + 1), jax.random.fold_in(arg_keys[2], 1), PANEL // 2, PANEL).astype(jnp.int32),
        "gain_in": jnp.clip(1.0 + 0.18 * jax.random.normal(arg_keys[3], (D,), jnp.float32), 0.1, 1.9),
        "kv_down": gaussian(arg_keys[4], (D, KV), D ** -0.5, 0.0625, ((0, 4),)),
        "gain_latent": jnp.clip(1.0 + 0.18 * jax.random.normal(arg_keys[5], (KV,), jnp.float32), 0.1, 1.9),
        "cotangent": heavy_noise(arg_keys[6], (GROUPS, REACH, SLOTS, PANEL, KV), (2 * (PANELS * PANEL) ** -0.5), 0.25, ((0, 256),), (0, 4, 256, 6.0)),
    }


epsilon = 1e-06

def finish(raw, gain_latent, cotangent_rows, valid_mask):
    rms_lat = jnp.sqrt(lax.optimization_barrier(jnp.mean(raw * raw, axis=-1)) + epsilon)
    unit_rows = raw / rms_lat[:, None]
    normed = (unit_rows * gain_latent * valid_mask[:, None]).astype(jnp.bfloat16)
    weighted = gain_latent * (cotangent_rows.astype(jnp.float32) * valid_mask[:, None])
    latent_grad = (weighted - unit_rows * lax.optimization_barrier(jnp.mean(unit_rows * weighted, axis=-1, keepdims=True))) / rms_lat[:, None]
    backward = latent_grad.astype(jnp.bfloat16)
    return (normed, backward)

def reference(hidden, routes, counts, gain_in, kv_down, gain_latent, cotangent):
    panels = hidden.reshape(GROUPS, SLOTS, PANEL, D)
    server_ids = jnp.arange(GROUPS, dtype=jnp.int32)
    trainer_ids = ((server_ids[:, None] + routes) % GROUPS).astype(jnp.int32)
    slot_ids = jnp.broadcast_to(jnp.arange(SLOTS, dtype=jnp.int32)[None, :], (GROUPS, SLOTS))
    picked = cotangent[trainer_ids, routes, slot_ids]

    def server_step(total, inputs):
        blocks, limits, cotangents = inputs
        widened = blocks.reshape(SLOTS * PANEL, D).astype(jnp.float32)
        scaled = (widened * gain_in).astype(jnp.bfloat16)
        raw = jnp.dot(scaled, kv_down, preferred_element_type=jnp.float32)
        position = lax.broadcasted_iota(jnp.int32, (SLOTS, PANEL), 1)
        valid_mask = (position < limits[:, None]).astype(jnp.float32).reshape(SLOTS * PANEL)
        normed, backward = finish(raw, gain_latent, cotangents.reshape(SLOTS * PANEL, KV), valid_mask)
        total = total + jnp.dot(backward.T, scaled, preferred_element_type=jnp.float32)
        return (total, normed.reshape(SLOTS, PANEL, KV))
    start_total = jnp.zeros((KV, D), jnp.float32)
    gradient, normed_all = lax.scan(server_step, start_total, (panels, counts, picked))
    latent = jnp.zeros((GROUPS, REACH, SLOTS, PANEL, KV), jnp.bfloat16)
    latent = latent.at[trainer_ids, routes, slot_ids].set(normed_all)
    return (latent, gradient)
```

```python
import jax
import jax.numpy as jnp
from jax import lax
from jax.sharding import PartitionSpec as P

epsilon = 1e-06
Y, Z, C, X = "y", "z", "c", "x"
f32, bf16 = jnp.float32, jnp.bfloat16


def chip_shift(shard, by):
    devices = lax.axis_size((Y, Z, C))
    pairs = [(i, (i + 2 * by) % devices) for i in range(devices)]
    return lax.ppermute(shard, (Y, Z, C), pairs)


def finish(raw, gain_latent, cotangent_rows, valid_mask):
    rms_lat = jnp.sqrt(jnp.mean(raw * raw, axis=-1) + epsilon)
    unit_rows = raw / rms_lat[:, None]
    normed = (unit_rows * gain_latent * valid_mask[:, None]).astype(bf16)
    weighted = gain_latent * (cotangent_rows.astype(f32) * valid_mask[:, None])
    latent_grad = (
        weighted - unit_rows * jnp.mean(unit_rows * weighted, axis=-1, keepdims=True)
    ) / rms_lat[:, None]
    return normed, latent_grad.astype(bf16)


def body(hidden, routes, counts, gain_in, kv_down, gain_latent, cotangent):
    panel_len, width = hidden.shape[1], hidden.shape[2]
    latent_width = kv_down.shape[1]
    ny, nz, nc, nx = (lax.axis_size(a) for a in (Y, Z, C, X))
    core = lax.axis_index(C)
    route = routes[0, 0]
    count = counts[0, 0]
    cot = cotangent.reshape(3, panel_len, latent_width)

    with jax.named_scope("share_core"):
        pair_hidden = lax.all_gather(hidden[0], C, axis=0, tiled=True)
        pair_cot1 = lax.all_gather(cot[1], C, axis=0, tiled=False)
    with jax.named_scope("cotangent_back"):
        came = chip_shift(jnp.stack([pair_cot1[0], cot[2]]), -1)

    with jax.named_scope("project"):
        scaled = (pair_hidden.astype(f32) * gain_in).astype(bf16)
        own = (hidden[0].astype(f32) * gain_in).astype(bf16)
        partial_raw = jnp.dot(own, kv_down, preferred_element_type=f32)
        spread = jnp.broadcast_to(partial_raw, (nx,) + partial_raw.shape)
    with jax.named_scope("sum_x"):
        raw = jnp.sum(lax.all_to_all(spread, X, 0, 0), axis=0)

    with jax.named_scope("finish"):
        position = lax.broadcasted_iota(jnp.int32, (panel_len,), 0)
        valid_mask = (position < count).astype(f32)
        cot1 = jnp.where(core == 0, pair_cot1[1], came[0])
        picked = jnp.where(route == 0, cot[0], jnp.where(route == 1, cot1, came[1]))
        normed, backward = finish(raw, gain_latent, picked, valid_mask)
        none = jnp.zeros_like(normed)
        slot0, sent1, sent2 = (jnp.where(route == o, normed, none) for o in range(3))

    with jax.named_scope("share_backward"):
        pair = lax.all_gather(jnp.stack([backward, sent1]), C, axis=0, tiled=False)
    with jax.named_scope("latent_out"):
        arrived = chip_shift(jnp.stack([pair[1, 1], sent2]), 1)

    with jax.named_scope("gradient"):
        rows = latent_width // nc
        shape = (latent_width, rows)
        pick = (
            lax.broadcasted_iota(jnp.int32, shape, 0)
            == nc * lax.broadcasted_iota(jnp.int32, shape, 1) + core
        ).astype(bf16)
        pair_backward = pair[:, 0].reshape(nc * panel_len, latent_width)
        mine = jnp.dot(pair_backward, pick, preferred_element_type=f32).astype(bf16)
        total = lax.dot_general(
            mine, scaled, (((0,), (0,)), ((), ())), preferred_element_type=f32
        )
    with jax.named_scope("sum_y"):
        sent = total.astype(bf16).reshape(ny, nz, width)
        over_y = jnp.sum(lax.all_to_all(sent, Y, 0, 0).astype(f32), axis=0)
    with jax.named_scope("sum_z"):
        lanes = over_y.reshape(nz, width // 128, 128)
        over_z = jnp.sum(lax.all_to_all(lanes, Z, 0, 0), axis=0)
        gradient = over_z.reshape(1, width)

    slot1 = jnp.where(core == 0, arrived[0], pair[0, 1])
    latent = jnp.stack([slot0, slot1, arrived[1]]).reshape(cotangent.shape)
    return latent, gradient


def solution(mesh):
    shape = dict(mesh.shape)
    tp = shape["tp"]
    ny, nz = 8, 16
    nc = shape["dp"] // (ny * nz)
    split = jax.sharding.Mesh(mesh.devices.reshape(ny, nz, nc, tp), (Y, Z, C, X))
    dp = (Y, Z, C)
    in_specs = (
        P(dp, None, X),
        P(dp, None),
        P(dp, None),
        P(X),
        P(X, None),
        P(),
        P(dp, None, None, None, None),
    )
    out_specs = (P(dp, None, None, None, None), P(dp, X))
    return jax.shard_map(body, mesh=split, in_specs=in_specs, out_specs=out_specs, check_vma=False)
```

```python
import jax
import jax.numpy as jnp
from jax import lax
from jax.sharding import PartitionSpec as P

epsilon = 1e-06
Y, Z, C, X = "y", "z", "c", "x"
f32, bf16 = jnp.float32, jnp.bfloat16


def along_dp(shard, by):
    devices = lax.axis_size((Y, Z, C))
    pairs = [(i, (i + by) % devices) for i in range(devices)]
    return lax.ppermute(shard, (Y, Z, C), pairs)


def mixed(rank, size):
    up, down = size // 2 + rank // 2, size // 2 - 1 - rank // 2
    odd = rank % 2
    return up * (1 - odd) + down * odd


def other_core(shard):
    return lax.ppermute(shard, C, [(0, 1), (1, 0)])


def finish(raw, gain_latent, cotangent_rows, valid_mask):
    rms_lat = jnp.sqrt(jnp.mean(raw * raw, axis=-1) + epsilon)
    unit_rows = raw / rms_lat[:, None]
    normed = (unit_rows * gain_latent * valid_mask[:, None]).astype(bf16)
    weighted = gain_latent * (cotangent_rows.astype(f32) * valid_mask[:, None])
    latent_grad = (
        weighted - unit_rows * jnp.mean(unit_rows * weighted, axis=-1, keepdims=True)
    ) / rms_lat[:, None]
    return normed, latent_grad.astype(bf16)


def body(hidden, routes, counts, gain_in, kv_down, gain_latent, cotangent):
    panel_len, width = hidden.shape[1], hidden.shape[2]
    latent_width = kv_down.shape[1]
    ny, nz, nc, nx = (lax.axis_size(a) for a in (Y, Z, C, X))
    core = lax.axis_index(C)
    route = routes[0, 0]
    count = counts[0, 0]
    cot = cotangent.reshape(3, panel_len, latent_width)

    with jax.named_scope("project"):
        own_scaled = (hidden[0].astype(f32) * gain_in).astype(bf16)
        partial_raw = jnp.dot(own_scaled, kv_down, preferred_element_type=f32)
        spread = jnp.broadcast_to(partial_raw, (nx,) + partial_raw.shape)
    with jax.named_scope("after_project"):
        spread, cot_none, cot_one, cot_two, hidden_sent = lax.optimization_barrier(
            (spread, cot[0], cot[1], cot[2], hidden[0])
        )
    with jax.named_scope("sum_x"):
        raw = jnp.sum(lax.all_to_all(spread, X, 0, 0), axis=0)
    with jax.named_scope("cotangent_back"):
        came1 = along_dp(cot_one, -1)
        came2 = along_dp(cot_two, -2)
    with jax.named_scope("share_hidden"):
        pair_hidden = other_core(hidden_sent)

    with jax.named_scope("finish"):
        position = lax.broadcasted_iota(jnp.int32, (panel_len,), 0)
        valid_mask = (position < count).astype(f32)
        picked = jnp.where(route == 0, cot_none, jnp.where(route == 1, came1, came2))
        normed, backward = finish(raw, gain_latent, picked, valid_mask)
        none = jnp.zeros_like(normed)
        slot0, sent1, sent2 = (jnp.where(route == o, normed, none) for o in range(3))

    with jax.named_scope("share_backward"):
        pair_backward = other_core(backward)

    with jax.named_scope("gradient"):
        rows = latent_width // nc
        shape = (latent_width, rows)
        place = lax.broadcasted_iota(jnp.int32, shape, 1)
        turned_row = mixed(place // nz, ny) * nz + place % nz
        pick = (
            lax.broadcasted_iota(jnp.int32, shape, 0)
            == nc * turned_row + core
        ).astype(bf16)

        def part(back, scaled):
            mine = jnp.dot(back, pick, preferred_element_type=f32).astype(bf16)
            return lax.dot_general(
                mine, scaled, (((0,), (0,)), ((), ())), preferred_element_type=f32
            )

        pair_scaled = (pair_hidden.astype(f32) * gain_in).astype(bf16)
        total = part(backward, own_scaled) + part(pair_backward, pair_scaled)
        sent = total.astype(bf16).reshape(ny, nz, width)
    with jax.named_scope("after_gradient"):
        sent, sent1, sent2 = lax.optimization_barrier((sent, sent1, sent2))
    with jax.named_scope("sum_y"):
        turned = [[int(mixed(r, ny)) for r in range(ny)]]
        came_y = lax.all_to_all(sent, Y, 0, 0, axis_index_groups=turned)
        over_y = jnp.sum(came_y.astype(f32), axis=0)
    with jax.named_scope("latent_out"):
        slot1 = along_dp(sent1, 1)
        slot2 = along_dp(sent2, 2)
    latent = jnp.stack([slot0, slot1, slot2]).reshape(cotangent.shape)
    with jax.named_scope("sum_z"):
        lanes = over_y.reshape(nz, width // 256, 256).astype(bf16)
        lanes, latent = lax.optimization_barrier((lanes, latent))
        over_z = jnp.sum(lax.all_to_all(lanes, Z, 0, 0).astype(f32), axis=0)
        gradient = over_z.reshape(1, width)

    return latent, gradient


def solution(mesh):
    shape = dict(mesh.shape)
    tp = shape["tp"]
    ny, nz = 8, 16
    nc = shape["dp"] // (ny * nz)
    split = jax.sharding.Mesh(mesh.devices.reshape(ny, nz, nc, tp), (Y, Z, C, X))
    dp = (Y, Z, C)
    in_specs = (
        P(dp, None, X),
        P(dp, None),
        P(dp, None),
        P(X),
        P(X, None),
        P(),
        P(dp, None, None, None, None),
    )
    out_specs = (P(dp, None, None, None, None), P(dp, X))
    return jax.shard_map(body, mesh=split, in_specs=in_specs, out_specs=out_specs, check_vma=False)
```

```python
import jax
import jax.numpy as jnp
from jax import lax
from jax.sharding import PartitionSpec as P

epsilon = 1e-06
Y, Z, C, X = "y", "z", "c", "x"
f32, bf16 = jnp.float32, jnp.bfloat16


def along_dp(shard, by):
    devices = lax.axis_size((Y, Z, C))
    pairs = [(i, (i + by) % devices) for i in range(devices)]
    return lax.ppermute(shard, (Y, Z, C), pairs)


def ordered(rank, size):
    half = size // 2
    late = rank // half
    return (half + rank) * (1 - late) + (size - 1 - rank) * late


def other_core(shard):
    return lax.ppermute(shard, C, [(0, 1), (1, 0)])


def finish(raw, gain_latent, cotangent_rows, valid_mask):
    rms_lat = jnp.sqrt(jnp.mean(raw * raw, axis=-1) + epsilon)
    unit_rows = raw / rms_lat[:, None]
    normed = (unit_rows * gain_latent * valid_mask[:, None]).astype(bf16)
    weighted = gain_latent * (cotangent_rows.astype(f32) * valid_mask[:, None])
    latent_grad = (
        weighted - unit_rows * jnp.mean(unit_rows * weighted, axis=-1, keepdims=True)
    ) / rms_lat[:, None]
    return normed, latent_grad.astype(bf16)


def body(hidden, routes, counts, gain_in, kv_down, gain_latent, cotangent):
    panel_len, width = hidden.shape[1], hidden.shape[2]
    latent_width = kv_down.shape[1]
    ny, nz, nc, nx = (lax.axis_size(a) for a in (Y, Z, C, X))
    core = lax.axis_index(C)
    route = routes[0, 0]
    count = counts[0, 0]
    cot = cotangent.reshape(3, panel_len, latent_width)

    with jax.named_scope("project"):
        own_scaled = (hidden[0].astype(f32) * gain_in).astype(bf16)
        partial_raw = jnp.dot(own_scaled, kv_down, preferred_element_type=f32)
        spread = jnp.broadcast_to(partial_raw, (nx,) + partial_raw.shape)
    with jax.named_scope("after_project"):
        spread, cot_none, cot_one, cot_two, hidden_sent = lax.optimization_barrier(
            (spread, cot[0], cot[1], cot[2], hidden[0])
        )
    with jax.named_scope("sum_x"):
        raw = jnp.sum(lax.all_to_all(spread, X, 0, 0), axis=0)
    with jax.named_scope("cotangent_back"):
        came1 = along_dp(cot_one, -1)
        came2 = along_dp(cot_two, -2)
        gain_rows = jnp.broadcast_to(gain_latent, (8, latent_width))
        came1, gain_rows = lax.optimization_barrier((came1, gain_rows))
    with jax.named_scope("share_hidden"):
        pair_hidden = other_core(hidden_sent)

    with jax.named_scope("finish"):
        position = lax.broadcasted_iota(jnp.int32, (panel_len,), 0)
        valid_mask = (position < count).astype(f32)
        picked = jnp.where(route == 0, cot_none, jnp.where(route == 1, came1, came2))
        normed, backward = finish(raw, gain_rows[0], picked, valid_mask)
        none = jnp.zeros_like(normed)
        slot0, sent1, sent2 = (jnp.where(route == o, normed, none) for o in range(3))

    with jax.named_scope("share_backward"):
        pair_backward = other_core(backward)

    with jax.named_scope("gradient"):
        rows = latent_width // nc
        shape = (latent_width, rows)
        place = lax.broadcasted_iota(jnp.int32, shape, 1)
        turned_row = ordered(place // nz, ny) * nz + place % nz
        pick = (
            lax.broadcasted_iota(jnp.int32, shape, 0)
            == nc * turned_row + core
        ).astype(bf16)

        def part(back, scaled):
            mine = jnp.dot(back, pick, preferred_element_type=f32).astype(bf16)
            return lax.dot_general(
                mine, scaled, (((0,), (0,)), ((), ())), preferred_element_type=f32
            )

        pair_scaled = (pair_hidden.astype(f32) * gain_in).astype(bf16)
        total = part(backward, own_scaled) + part(pair_backward, pair_scaled)
        sent = total.astype(bf16).reshape(ny, nz, width)
    with jax.named_scope("after_gradient"):
        sent, sent1, sent2 = lax.optimization_barrier((sent, sent1, sent2))
    with jax.named_scope("sum_y"):
        turned = [[int(ordered(r, ny)) for r in range(ny)]]
        came_y = lax.all_to_all(sent, Y, 0, 0, axis_index_groups=turned)
        over_y = jnp.sum(came_y.astype(f32), axis=0)
    with jax.named_scope("latent_out"):
        slot1 = along_dp(sent1, 1)
        slot2 = along_dp(sent2, 2)
    latent = jnp.stack([slot0, slot1, slot2]).reshape(cotangent.shape)
    with jax.named_scope("sum_z"):
        lanes = over_y.reshape(nz, width // 256, 256).astype(bf16)
        lanes, latent = lax.optimization_barrier((lanes, latent))
        over_z = jnp.sum(lax.all_to_all(lanes, Z, 0, 0).astype(f32), axis=0)
        gradient = over_z.reshape(1, width)

    return latent, gradient


def solution(mesh):
    shape = dict(mesh.shape)
    tp = shape["tp"]
    ny, nz = 8, 16
    nc = shape["dp"] // (ny * nz)
    split = jax.sharding.Mesh(mesh.devices.reshape(ny, nz, nc, tp), (Y, Z, C, X))
    dp = (Y, Z, C)
    in_specs = (
        P(dp, None, X),
        P(dp, None),
        P(dp, None),
        P(X),
        P(X, None),
        P(),
        P(dp, None, None, None, None),
    )
    out_specs = (P(dp, None, None, None, None), P(dp, X))
    return jax.shard_map(body, mesh=split, in_specs=in_specs, out_specs=out_specs, check_vma=False)
```

```python
import jax
import jax.numpy as jnp
from jax import lax
from jax.sharding import PartitionSpec as P

epsilon = 1e-06
Y, Z, C, X = "y", "z", "c", "x"
f32, bf16 = jnp.float32, jnp.bfloat16


def along_dp(shard, by):
    devices = lax.axis_size((Y, Z, C))
    pairs = [(i, (i + by) % devices) for i in range(devices)]
    return lax.ppermute(shard, (Y, Z, C), pairs)


def ordered(rank, size):
    half = size // 2
    late = rank // half
    return (half + rank) * (1 - late) + (size - 1 - rank) * late


def other_core(shard):
    return lax.ppermute(shard, C, [(0, 1), (1, 0)])


def finish(raw, gain_latent, cotangent_rows, valid_mask):
    rms_lat = jnp.sqrt(jnp.mean(raw * raw, axis=-1) + epsilon)
    unit_rows = raw / rms_lat[:, None]
    normed = (unit_rows * gain_latent * valid_mask[:, None]).astype(bf16)
    weighted = gain_latent * (cotangent_rows.astype(f32) * valid_mask[:, None])
    latent_grad = (
        weighted - unit_rows * jnp.mean(unit_rows * weighted, axis=-1, keepdims=True)
    ) / rms_lat[:, None]
    return normed, latent_grad.astype(bf16)


def body(hidden, routes, counts, gain_in, kv_down, gain_latent, cotangent):
    panel_len, width = hidden.shape[1], hidden.shape[2]
    latent_width = kv_down.shape[1]
    ny, nz, nc, nx = (lax.axis_size(a) for a in (Y, Z, C, X))
    core = lax.axis_index(C)
    route = routes[0, 0]
    count = counts[0, 0]
    cot = cotangent.reshape(3, panel_len, latent_width)

    with jax.named_scope("project"):
        own_scaled = (hidden[0].astype(f32) * gain_in).astype(bf16)
        partial_raw = jnp.dot(own_scaled, kv_down, preferred_element_type=f32)
        spread = jnp.broadcast_to(partial_raw, (nx,) + partial_raw.shape)
    with jax.named_scope("after_project"):
        spread, cot_none, cot_one, cot_two, hidden_sent = lax.optimization_barrier(
            (spread, cot[0], cot[1], cot[2], hidden[0])
        )
    with jax.named_scope("sum_x"):
        raw = jnp.sum(lax.all_to_all(spread, X, 0, 0), axis=0)
    with jax.named_scope("cotangent_back"):
        came1 = along_dp(cot_one, -1)
        came2 = along_dp(cot_two, -2)
        gain_rows = jnp.broadcast_to(gain_latent, (8, latent_width))
        came1, gain_rows = lax.optimization_barrier((came1, gain_rows))
    with jax.named_scope("share_hidden"):
        pair_hidden = lax.all_gather(hidden_sent, C, axis=0, tiled=True)

    with jax.named_scope("finish"):
        position = lax.broadcasted_iota(jnp.int32, (panel_len,), 0)
        valid_mask = (position < count).astype(f32)
        picked = jnp.where(route == 0, cot_none, jnp.where(route == 1, came1, came2))
        normed, backward = finish(raw, gain_rows[0], picked, valid_mask)
        none = jnp.zeros_like(normed)
        slot0, sent1, sent2 = (jnp.where(route == o, normed, none) for o in range(3))

    with jax.named_scope("share_backward"):
        pair_backward = lax.all_gather(backward, C, axis=0, tiled=True)

    with jax.named_scope("gradient"):
        rows = latent_width // nc
        shape = (latent_width, rows)
        place = lax.broadcasted_iota(jnp.int32, shape, 1)
        turned_row = ordered(place // nz, ny) * nz + place % nz
        pick = (
            lax.broadcasted_iota(jnp.int32, shape, 0)
            == nc * turned_row + core
        ).astype(bf16)

        def part(back, scaled):
            mine = jnp.dot(back, pick, preferred_element_type=f32).astype(bf16)
            return lax.dot_general(
                mine, scaled, (((0,), (0,)), ((), ())), preferred_element_type=f32
            )

        pair_scaled = (pair_hidden.astype(f32) * gain_in).astype(bf16)
        total = part(pair_backward, pair_scaled)
        sent = total.astype(bf16).reshape(ny, nz, width)
    with jax.named_scope("after_gradient"):
        sent, sent1, sent2 = lax.optimization_barrier((sent, sent1, sent2))
    with jax.named_scope("sum_y"):
        turned = [[int(ordered(r, ny)) for r in range(ny)]]
        came_y = lax.all_to_all(sent, Y, 0, 0, axis_index_groups=turned)
        over_y = jnp.sum(came_y.astype(f32), axis=0)
    with jax.named_scope("latent_out"):
        slot1 = along_dp(sent1, 1)
        slot2 = along_dp(sent2, 2)
    latent = jnp.stack([slot0, slot1, slot2]).reshape(cotangent.shape)
    with jax.named_scope("sum_z"):
        lanes = over_y.reshape(nz, width // 256, 256).astype(bf16)
        lanes, latent = lax.optimization_barrier((lanes, latent))
        over_z = jnp.sum(lax.all_to_all(lanes, Z, 0, 0).astype(f32), axis=0)
        gradient = over_z.reshape(1, width)

    return latent, gradient


def solution(mesh):
    shape = dict(mesh.shape)
    tp = shape["tp"]
    ny, nz = 8, 16
    nc = shape["dp"] // (ny * nz)
    split = jax.sharding.Mesh(mesh.devices.reshape(ny, nz, nc, tp), (Y, Z, C, X))
    dp = (Y, Z, C)
    in_specs = (
        P(dp, None, X),
        P(dp, None),
        P(dp, None),
        P(X),
        P(X, None),
        P(),
        P(dp, None, None, None, None),
    )
    out_specs = (P(dp, None, None, None, None), P(dp, X))
    return jax.shard_map(body, mesh=split, in_specs=in_specs, out_specs=out_specs, check_vma=False)
```
